128 devices in a mesh: row: 8 (over z_hi, y), col: 16 (over z_lo, x, core).
Axes of the slice: x: 4, y: 4, z: 4 (z_hi: 2, z_lo: 2; z = z_hi * 2 + z_lo), core: 2. Of those that a mesh axis runs over, the one named last changes fastest.
Arguments:
- tokens: bfloat16 [1024, 16384], P('col', 'row'), may hold values from -6 to 6
- dropout_keep_mask: int32 [1024, 16384], P('col', 'row'), may hold values 0 or 1
- frozen_gate_weight: bfloat16 [16384, 16384], P('row', 'col'), may hold values from -0.046875 to 0.046875
- frozen_up_weight: bfloat16 [16384, 16384], P('row', 'col'), may hold values from -0.046875 to 0.046875
- down_weight: bfloat16 [16384, 16384], P('col', 'row'), may hold values from -0.046875 to 0.046875
- adapter_input_maps: bfloat16 [32, 16384], P(None, 'row'), may hold values from -0.046875 to 0.046875
- adapter_output_maps: bfloat16 [2, 16, 16384], P(None, None, 'col'), may hold values from -1.5 to 1.5
- out_grad: bfloat16 [1024, 16384], P('col', 'row'), may hold values from -6 to 6
Outputs:
- mixed_out: bfloat16 [1024, 16384], P('col', 'row')
- token_input_gradient: bfloat16 [1024, 16384], P('col', 'row')
- grad_adapt_in: float32 [32, 16384], P(None, 'row')
- adapter_output_gradient: float32 [2, 16, 16384], P(None, None, 'col')
The draws below stay inside these ranges and needn't reach their ends.
All inputs are finite; a program needn't handle non-finite values. No bound on the sum of `dropout_keep_mask` on one device may be relied on, other than what follows from the above.
Results may differ from the reference program's by a relative error of at most 0.033.
Values may be sent and summed in bfloat16 or wider, within the bound.
No kernel may reach another device: no remote copies, remote signals or barrier semaphores. Data moves between devices by JAX's collectives and lax.ppermute only.
A program may use at most 128 MiB of HBM per device.

```python
import jax
import jax.numpy as jnp
from jax import lax

D = 16384
FF = 16384
LOW_RANK = 16
TOKENS = 1024
N_ROW = 8
N_COL = 16


def place_ends(array, key, low, high):
    longest = array.shape.index(max(array.shape))
    spots = []
    for shift in (0, 1):
        where = [jax.random.randint(jax.random.fold_in(key, axis), (), 0, length) for axis, length in enumerate(array.shape)]
        where[longest] = (where[longest] + shift) % array.shape[longest]
        spots.append(tuple(where))
    return array.at[spots[0]].set(low).at[spots[1]].set(high)


def shard_levels(own_key, shape, pieces, smallest, largest):
    gain = 1.0
    for axis_at, parts in pieces:
        heights = jax.random.uniform(jax.random.fold_in(jax.random.fold_in(own_key, 6), axis_at), (parts,), jnp.float32, smallest / len(pieces), largest / len(pieces))
        gain = gain * jnp.repeat(jnp.exp(heights), shape[axis_at] // parts).reshape((-1,) + (1,) * (len(shape) - 1 - axis_at))
    return gain


def gaussian(rng, shape, spread, limit, pieces=(), kind=jnp.bfloat16):
    array = jax.random.normal(rng, shape, jnp.float32) * spread
    if len(pieces) > 0:
        array = shard_levels(rng, shape, pieces, -0.22, 0.18) * array
    return jnp.clip(array, min=-limit, max=limit).astype(kind)


def setup_inputs(seed: int = 0) -> dict:
    seeds = jax.random.split(jax.random.key(seed), 9)
    return {
        "tokens": gaussian(seeds[0], (TOKENS, D), 1.0, 6.0, ((0, 16), (1, 8))),
        "dropout_keep_mask": place_ends((jax.random.randint(seeds[1], (TOKENS, D), 0, 10) < 9).astype(jnp.int32), jax.random.fold_in(seeds[1], 1), 0, 1),
        "frozen_gate_weight": gaussian(seeds[2], (D, FF), D ** -0.5, 0.046875, ((0, 8), (1, 16))),
        "frozen_up_weight": gaussian(seeds[3], (D, FF), D ** -0.5, 0.046875, ((0, 8), (1, 16))),
        "down_weight": gaussian(seeds[4], (FF, D), FF ** -0.5, 0.046875, ((0, 16), (1, 8))),
        "adapter_input_maps": gaussian(seeds[5], (2 * LOW_RANK, D), D ** -0.5, 0.046875, ((1, 8),)),
        "adapter_output_maps": gaussian(seeds[6], (2, LOW_RANK, FF), LOW_RANK ** -0.5, 1.5, ((2, 16),)),
        "out_grad": gaussian(seeds[7], (TOKENS, D), 1.0, 6.0, ((0, 16), (1, 8))),
    }


keep_scale = 10.0 / 9.0
adapter_scale = 0.5


def matmul_left_transposed(left, right):
    return lax.dot_general(left, right, (((0,), (0,)), ((), ())), preferred_element_type=jnp.float32)


def matmul_right_transposed(left, right):
    return lax.dot_general(left, right, (((1,), (1,)), ((), ())), preferred_element_type=jnp.float32)


def rounded_sum(term, count, width, shape):
    def step(total, index):
        start = (index * width).astype(jnp.int32)
        part = term(start, width).astype(jnp.bfloat16)
        part = lax.optimization_barrier(part)
        return total + part.astype(jnp.float32), None

    total, unused = lax.scan(step, jnp.zeros(shape, jnp.float32), jnp.arange(count, dtype=jnp.int32))
    return total


def reference(tokens, dropout_keep_mask, frozen_gate_weight, frozen_up_weight, down_weight, adapter_input_maps, adapter_output_maps, out_grad):
    row_width = D // N_ROW
    col_width = FF // N_COL
    dropped = tokens * dropout_keep_mask.astype(jnp.bfloat16)
    reduced_features = (matmul_right_transposed(dropped, adapter_input_maps) * keep_scale).astype(jnp.bfloat16)

    def frozen_input_weight(weight):
        def term(start, width):
            return jnp.dot(lax.dynamic_slice_in_dim(tokens, start, width, 1), lax.dynamic_slice_in_dim(weight, start, width, 0), preferred_element_type=jnp.float32)
        return rounded_sum(term, N_ROW, row_width, (TOKENS, FF))

    gate_activation = frozen_input_weight(frozen_gate_weight) + adapter_scale * jnp.dot(reduced_features[:, :LOW_RANK], adapter_output_maps[0], preferred_element_type=jnp.float32)
    up_activation = frozen_input_weight(frozen_up_weight) + adapter_scale * jnp.dot(reduced_features[:, LOW_RANK:], adapter_output_maps[1], preferred_element_type=jnp.float32)
    sigmoid_gate = jax.nn.sigmoid(gate_activation)
    activated = gate_activation * sigmoid_gate
    hidden = (activated * up_activation).astype(jnp.bfloat16)

    def mixed_term(start, width):
        return jnp.dot(lax.dynamic_slice_in_dim(hidden, start, width, 1), lax.dynamic_slice_in_dim(down_weight, start, width, 0), preferred_element_type=jnp.float32)

    mixed_out = rounded_sum(mixed_term, N_COL, col_width, (TOKENS, D)).astype(jnp.bfloat16)

    def back_term(start, width):
        return matmul_right_transposed(lax.dynamic_slice_in_dim(out_grad, start, width, 1), lax.dynamic_slice_in_dim(down_weight, start, width, 1))

    hidden_grad = rounded_sum(back_term, N_ROW, row_width, (TOKENS, FF))
    gate_gradient = (hidden_grad * up_activation * sigmoid_gate * (1.0 + gate_activation * (1.0 - sigmoid_gate))).astype(jnp.bfloat16)
    up_gradient = (hidden_grad * activated).astype(jnp.bfloat16)
    reduced_gradient = adapter_scale * jnp.concatenate([matmul_right_transposed(gate_gradient, adapter_output_maps[0]), matmul_right_transposed(up_gradient, adapter_output_maps[1])], axis=1)
    scaled_product = (reduced_gradient * keep_scale).astype(jnp.bfloat16)
    adapter_output_gradient = adapter_scale * jnp.stack([matmul_left_transposed(reduced_features[:, :LOW_RANK], gate_gradient), matmul_left_transposed(reduced_features[:, LOW_RANK:], up_gradient)])
    grad_adapt_in = matmul_left_transposed(scaled_product, dropped)

    def input_term(start, width):
        first = matmul_right_transposed(lax.dynamic_slice_in_dim(gate_gradient, start, width, 1), lax.dynamic_slice_in_dim(frozen_gate_weight, start, width, 1))
        second = matmul_right_transposed(lax.dynamic_slice_in_dim(up_gradient, start, width, 1), lax.dynamic_slice_in_dim(frozen_up_weight, start, width, 1))
        return first + second

    frozen_output_part = rounded_sum(input_term, N_COL, col_width, (TOKENS, D))
    adapter_output_part = dropout_keep_mask.astype(jnp.float32) * jnp.dot(scaled_product, adapter_input_maps, preferred_element_type=jnp.float32)
    token_input_gradient = (frozen_output_part + adapter_output_part).astype(jnp.bfloat16)
    return mixed_out, token_input_gradient, grad_adapt_in, adapter_output_gradient
```

```python
import jax
import jax.numpy as jnp
from jax import lax
from jax.sharding import Mesh
from jax.sharding import PartitionSpec as P

keep_scale = 10.0 / 9.0
adapter_scale = 0.5

ROW = ("zh", "y")
COL = ("zl", "x", "c")
CHIPS = ("zl", "x")


def dot_f32(left, right):
    return jnp.dot(left, right, preferred_element_type=jnp.float32)


def dot_left_t(left, right):
    return lax.dot_general(
        left, right, (((0,), (0,)), ((), ())), preferred_element_type=jnp.float32
    )


def dot_right_t(left, right):
    return lax.dot_general(
        left, right, (((1,), (1,)), ((), ())), preferred_element_type=jnp.float32
    )


def after(value, *others):
    return lax.optimization_barrier((value, *others))[0]


def exchange(blocks, axes):
    return lax.all_to_all(blocks, axes, 0, 0, tiled=True)


def spread(block, axes, count):
    return exchange(jnp.broadcast_to(block[None], (count, *block.shape)), axes)


def sum_blocks(blocks):
    return jnp.sum(blocks.astype(jnp.float32), axis=0)


def swap_core(value):
    return lax.ppermute(value, "c", [(0, 1), (1, 0)])


def local(tokens, mask, w_gate, w_up, w_down, a_in, a_out, out_grad):
    bf16, f32 = jnp.bfloat16, jnp.float32
    core = lax.axis_index("c")
    row_index = lax.axis_index(ROW)
    col_index = lax.axis_index(COL)
    rank = a_out.shape[1]
    hidden_width = w_gate.shape[1]
    col_tokens, features = tokens.shape
    n_col, n_row = lax.axis_size(COL), lax.axis_size(ROW)
    n_chips = n_col // 2
    all_tokens = col_tokens * n_col
    row_tokens = all_tokens // n_row

    tokens_all = lax.all_gather(tokens, COL, axis=0, tiled=True)
    dropped = tokens * mask.astype(bf16)
    low_part = dot_right_t(dropped, a_in)
    out_grad = after(out_grad, low_part)
    out_grad_all = lax.all_gather(out_grad, COL, axis=0, tiled=True)
    low_local = (sum_blocks(spread(low_part, ROW, n_row)) * keep_scale).astype(bf16)
    low_all = spread(low_local, COL, n_col).reshape(all_tokens, 2 * rank)
    w_in = jnp.concatenate([w_gate, w_up], axis=1)

    partial_gu = dot_f32(tokens_all, w_in).astype(bf16)
    dropped_all = lax.all_gather(after(dropped, partial_gu), COL, axis=0, tiled=True)
    gate_up = sum_blocks(exchange(partial_gu.reshape(n_row, row_tokens, 2 * hidden_width), ROW))
    partial_dh = dot_right_t(out_grad_all, w_down).astype(bf16)
    hidden_grad = sum_blocks(exchange(partial_dh.reshape(n_row, row_tokens, hidden_width), ROW))

    low_used = lax.dynamic_slice_in_dim(low_all, row_index * row_tokens, row_tokens, 0)
    gate = gate_up[:, :hidden_width] + adapter_scale * dot_f32(low_used[:, :rank], a_out[0])
    up = gate_up[:, hidden_width:] + adapter_scale * dot_f32(low_used[:, rank:], a_out[1])
    sig = jax.nn.sigmoid(gate)
    act = gate * sig
    hidden = (act * up).astype(bf16)
    gate_grad = (hidden_grad * up * sig * (1.0 + gate * (1.0 - sig))).astype(bf16)
    up_grad = (hidden_grad * act).astype(bf16)

    hidden_all = spread(hidden, ROW, n_row).reshape(all_tokens, hidden_width)
    partial_out = dot_f32(hidden_all, w_down).astype(bf16)
    mixed_out = lax.psum_scatter(partial_out, COL, scatter_dimension=0, tiled=True)

    low_grad_part = adapter_scale * jnp.concatenate(
        [dot_right_t(gate_grad, a_out[0]), dot_right_t(up_grad, a_out[1])], axis=1
    )
    scaled = (sum_blocks(spread(low_grad_part, COL, n_col)) * keep_scale).astype(bf16)
    joined = jnp.concatenate(
        [gate_grad, up_grad, jnp.pad(scaled, ((0, 0), (0, 128 - 2 * rank)))], axis=1
    )
    joined_all = spread(joined, ROW, n_row).reshape(all_tokens, 2 * hidden_width + 128)
    scaled_all = joined_all[:, 2 * hidden_width : 2 * hidden_width + 2 * rank]
    grads_all = joined_all[:, : 2 * hidden_width]

    by_core = grads_all.reshape(n_chips, 2, col_tokens, 2 * hidden_width)
    half = n_chips * col_tokens

    def input_part(which):
        rows = lax.dynamic_index_in_dim(by_core, which, 1, False).reshape(half, 2 * hidden_width)
        return dot_right_t(rows, w_in)

    away = swap_core(input_part(1 - core).astype(bf16))
    chip_sum = (input_part(core) + away.astype(f32)).astype(bf16)
    frozen_part = sum_blocks(exchange(chip_sum.reshape(n_chips, col_tokens, features), CHIPS))
    scaled_own = lax.dynamic_slice_in_dim(scaled_all, col_index * col_tokens, col_tokens, 0)
    adapter_part = mask.astype(f32) * dot_f32(scaled_own, a_in)
    token_input_gradient = (frozen_part + adapter_part).astype(bf16)

    grad_adapt_in = dot_left_t(scaled_all, dropped_all)
    adapter_output_gradient = adapter_scale * jnp.stack(
        [
            dot_left_t(low_all[:, :rank], grads_all[:, :hidden_width]),
            dot_left_t(low_all[:, rank:], grads_all[:, hidden_width:]),
        ]
    )
    return mixed_out, token_input_gradient, grad_adapt_in, adapter_output_gradient


def solution(mesh):
    split = Mesh(mesh.devices.reshape(2, 4, 2, 4, 2), (*ROW, *COL))
    both = P(COL, ROW)
    return jax.shard_map(
        local,
        mesh=split,
        in_specs=(
            both,
            both,
            P(ROW, COL),
            P(ROW, COL),
            both,
            P(None, ROW),
            P(None, None, COL),
            both,
        ),
        out_specs=(both, both, P(None, ROW), P(None, None, COL)),
        check_vma=False,
    )
```

```python
import jax
import jax.numpy as jnp
from jax import lax
from jax.sharding import Mesh
from jax.sharding import PartitionSpec as P

keep_scale = 10.0 / 9.0
adapter_scale = 0.5

ROW = ("zh", "y")
COL = ("zl", "x", "c")
CHIPS = ("zl", "x")


def dot_f32(left, right):
    return jnp.dot(left, right, preferred_element_type=jnp.float32)


def dot_left_t(left, right):
    return lax.dot_general(
        left, right, (((0,), (0,)), ((), ())), preferred_element_type=jnp.float32
    )


def dot_right_t(left, right):
    return lax.dot_general(
        left, right, (((1,), (1,)), ((), ())), preferred_element_type=jnp.float32
    )


def exchange(blocks, axes):
    return lax.all_to_all(blocks, axes, 0, 0, tiled=True)


def spread(block, axes, count):
    return exchange(jnp.broadcast_to(block[None], (count, *block.shape)), axes)


def sum_blocks(blocks):
    return jnp.sum(blocks.astype(jnp.float32), axis=0)


def trade(value, axis, bit):
    size = lax.axis_size(axis)
    return lax.ppermute(value, axis, [(i, i ^ bit) for i in range(size)])


def shift(value, axis, step):
    size = lax.axis_size(axis)
    return lax.ppermute(value, axis, [(i, (i + step) % size) for i in range(size)])


def sum_pairs(value, steps):
    for axis, bit in steps:
        both = value.astype(jnp.float32) + trade(value, axis, bit).astype(jnp.float32)
        value = both.astype(value.dtype)
    return value


ROW_PAIRS = (("y", 1), ("y", 2), ("zh", 1))
COL_PAIRS = (("c", 1), ("x", 1), ("x", 2), ("zl", 1))


def put(buffer, piece, index, axis, column=0):
    start = [0] * buffer.ndim
    start[axis], start[-1] = index, column
    return lax.dynamic_update_slice(buffer, jnp.expand_dims(piece, axis), start)


def gather_y(piece, axis):
    y, size = lax.axis_index("y"), lax.axis_size("y")
    half = piece.shape[-1] // 2
    behind, ahead = shift(piece, "y", 1), shift(piece, "y", -1)
    return gathered_y(piece, behind, ahead, axis)


def gathered_y(piece, behind, ahead, axis):
    y, size = lax.axis_index("y"), lax.axis_size("y")
    half = piece.shape[-1] // 2
    left = shift(behind[..., :half], "y", 1)
    right = shift(ahead[..., half:], "y", -1)
    shape = list(piece.shape)
    shape.insert(axis, size)
    buffer = jnp.zeros(shape, piece.dtype)
    buffer = put(buffer, piece, y, axis)
    buffer = put(buffer, behind, (y + 3) % size, axis)
    buffer = put(buffer, ahead, (y + 1) % size, axis)
    buffer = put(buffer, left, (y + 2) % size, axis)
    return put(buffer, right, (y + 2) % size, axis, half)


def scatter_y(first, second):
    y, size = lax.axis_index("y"), lax.axis_size("y")

    def pick(array, offset):
        return lax.dynamic_index_in_dim(array, (y + offset) % size, 1, False)

    def add(*terms):
        return sum(term.astype(jnp.float32) for term in terms)

    passed_up = shift(pick(first, 2), "y", 1)
    passed_down = shift(pick(second, 2), "y", -1)
    first_down = shift(pick(first, 3), "y", -1)
    second_up = shift(pick(second, 1), "y", 1)
    first_up = shift(add(pick(first, 1), passed_up).astype(first.dtype), "y", 1)
    second_down = shift(add(pick(second, 3), passed_down).astype(second.dtype), "y", -1)
    return (
        add(pick(first, 0), first_down, first_up),
        add(pick(second, 0), second_up, second_down),
    )


def scatter_zh(total):
    zh = lax.axis_index("zh")
    away = lax.dynamic_index_in_dim(total, 1 - zh, 0, False).astype(jnp.bfloat16)
    own = lax.dynamic_index_in_dim(total, zh, 0, False)
    return own + trade(away, "zh", 1).astype(jnp.float32)


def gather_x(piece):
    x, size = lax.axis_index("x"), lax.axis_size("x")
    behind, ahead, across = shift(piece, "x", 1), shift(piece, "x", -1), shift(piece, "x", 2)
    buffer = put(jnp.zeros((size, *piece.shape), piece.dtype), piece, x, 0)
    buffer = put(buffer, behind, (x + 3) % size, 0)
    buffer = put(buffer, ahead, (x + 1) % size, 0)
    return put(buffer, across, (x + 2) % size, 0)


def gather_col(block):
    zl, core = lax.axis_index("zl"), lax.axis_index("c")
    other = trade(block, "zl", 1)
    near = gather_x(block)
    far = gather_x(other)
    buffer = jnp.zeros((2, near.shape[0], 2, *block.shape), block.dtype)
    for rows, level in ((near, zl), (far, 1 - zl)):
        for half, side in ((rows, core), (trade(rows, "c", 1), 1 - core)):
            update = half[None, :, None]
            buffer = lax.dynamic_update_slice(buffer, update, (level, 0, side, 0, 0))
    return buffer, other


def join_zh(piece, axis):
    zh = lax.axis_index("zh")
    shape = list(piece.shape)
    shape.insert(axis, 2)
    other = trade(piece, "zh", 1)
    buffer = put(jnp.zeros(shape, piece.dtype), piece, zh, axis)
    return put(buffer, other, 1 - zh, axis)


def local(tokens, mask, w_gate, w_up, w_down, a_in, a_out, out_grad):
    bf16, f32 = jnp.bfloat16, jnp.float32
    core = lax.axis_index("c")
    row_index = lax.axis_index(ROW)
    col_index = lax.axis_index(COL)
    rank = a_out.shape[1]
    hidden_width = w_gate.shape[1]
    col_tokens, features = tokens.shape
    n_col, n_row = lax.axis_size(COL), lax.axis_size(ROW)
    n_chips = n_col // 2
    all_tokens = col_tokens * n_col
    row_tokens = all_tokens // n_row

    own_side = spread(tokens, CHIPS, n_chips)
    other_side = trade(own_side, "c", 1)
    tokens_all = jnp.stack(
        [jnp.where(core == 0, own_side, other_side), jnp.where(core == 0, other_side, own_side)],
        axis=1,
    ).reshape(all_tokens, features)
    dropped = tokens * mask.astype(bf16)
    low_part, own_side = lax.optimization_barrier((dot_right_t(dropped, a_in), own_side))
    low_local = (sum_blocks(spread(low_part, ROW, n_row)) * keep_scale).astype(bf16)
    low_all = spread(low_local, COL, n_col).reshape(all_tokens, 2 * rank)
    blocks = (2, n_row // 2, row_tokens)

    own_side, out_grad = lax.optimization_barrier((own_side, out_grad))
    out_grad_all = gather_col(out_grad)[0].reshape(all_tokens, features)
    gate_part = dot_f32(tokens_all, w_gate).astype(bf16).reshape(*blocks, hidden_width)
    up_part = dot_f32(tokens_all, w_up).astype(bf16).reshape(*blocks, hidden_width)
    gate_sum, up_sum = scatter_y(gate_part, up_part)
    grad_part = dot_right_t(out_grad_all, w_down).astype(bf16).reshape(*blocks, hidden_width)
    middle = hidden_width // 2
    grad_sums = scatter_y(grad_part[..., :middle], grad_part[..., middle:])
    hidden_grad = jnp.concatenate([scatter_zh(grad_sums[0]), scatter_zh(grad_sums[1])], axis=1)

    low_used = lax.dynamic_slice_in_dim(low_all, row_index * row_tokens, row_tokens, 0)
    gate = scatter_zh(gate_sum) + adapter_scale * dot_f32(low_used[:, :rank], a_out[0])
    up = scatter_zh(up_sum) + adapter_scale * dot_f32(low_used[:, rank:], a_out[1])
    sig = jax.nn.sigmoid(gate)
    act = gate * sig
    hidden = (act * up).astype(bf16)
    gate_grad = (hidden_grad * up * sig * (1.0 + gate * (1.0 - sig))).astype(bf16)
    up_grad = (hidden_grad * act).astype(bf16)
    joined = jnp.concatenate([gate_grad, up_grad], axis=1)

    def by_core(blocks):
        away = lax.dynamic_index_in_dim(blocks, 1 - core, -3, False)
        own = lax.dynamic_index_in_dim(blocks, core, -3, False)
        return jnp.stack([away, own])

    grads_pair = join_zh(by_core(joined.reshape(2, col_tokens, -1)), 1)
    grads_behind, grads_ahead = shift(grads_pair, "y", 1), shift(grads_pair, "y", -1)
    hidden_pieces = join_zh(gather_y(by_core(hidden.reshape(2, col_tokens, -1)), 1), 1)
    half_tokens = all_tokens // 2
    hidden_halves = hidden_pieces.reshape(2, half_tokens, hidden_width)

    low_grad_part = adapter_scale * jnp.concatenate(
        [dot_right_t(gate_grad, a_out[0]), dot_right_t(up_grad, a_out[1])], axis=1
    )
    low_grad_part, grads_behind, grads_ahead = lax.optimization_barrier(
        (low_grad_part, grads_behind, grads_ahead)
    )
    grads_pieces = gathered_y(grads_pair, grads_behind, grads_ahead, 2)
    grads_halves = grads_pieces.reshape(2, half_tokens, 2 * hidden_width)
    scaled = (sum_pairs(low_grad_part, COL_PAIRS) * keep_scale).astype(bf16)
    scaled_all = put(jnp.zeros((n_row, *scaled.shape), bf16), scaled, row_index, 0)
    scaled_all = sum_pairs(scaled_all, ROW_PAIRS).reshape(all_tokens, 2 * rank)
    scaled_own = lax.dynamic_slice_in_dim(scaled_all, col_index * col_tokens, col_tokens, 0)

    def over_chips(halves, product):
        away = trade(product(halves[0]).astype(bf16), "c", 1)
        own = lax.optimization_barrier(product(halves[1]).astype(bf16))
        chip_sum = (own.astype(f32) + away.astype(f32)).astype(bf16)
        return chip_sum.reshape(n_chips, col_tokens, features)

    mixed_sum = over_chips(hidden_halves, lambda rows: dot_f32(rows, w_down))

    adapt_part = dot_left_t(scaled_own, dropped).astype(bf16)
    adapter_part = mask.astype(f32) * dot_f32(scaled_own, a_in)
    adapt_sum = sum_pairs(adapt_part, COL_PAIRS)
    grads_halves, mixed_sum = lax.optimization_barrier((grads_halves, mixed_sum))
    mixed_out = sum_blocks(exchange(mixed_sum, CHIPS)).astype(bf16)
    w_in = jnp.concatenate([w_gate, w_up], axis=1)
    frozen_sum = over_chips(grads_halves, lambda rows: dot_right_t(rows, w_in))
    frozen_part = sum_blocks(exchange(frozen_sum, CHIPS))
    token_input_gradient = (frozen_part + adapter_part).astype(bf16)
    grad_adapt_in = adapt_sum.astype(f32)

    low_halves = by_core(low_all.reshape(n_chips, 2, col_tokens, 2 * rank))
    low_rows = low_halves.reshape(all_tokens, 2 * rank)
    grads_rows = grads_halves.reshape(all_tokens, 2 * hidden_width)
    adapter_output_gradient = adapter_scale * jnp.stack(
        [
            dot_left_t(low_rows[:, :rank], grads_rows[:, :hidden_width]),
            dot_left_t(low_rows[:, rank:], grads_rows[:, hidden_width:]),
        ]
    )
    return mixed_out, token_input_gradient, grad_adapt_in, adapter_output_gradient


def solution(mesh):
    split = Mesh(mesh.devices.reshape(2, 4, 2, 4, 2), (*ROW, *COL))
    both = P(COL, ROW)
    return jax.shard_map(
        local,
        mesh=split,
        in_specs=(
            both,
            both,
            P(ROW, COL),
            P(ROW, COL),
            both,
            P(None, ROW),
            P(None, None, COL),
            both,
        ),
        out_specs=(both, both, P(None, ROW), P(None, None, COL)),
        check_vma=False,
    )
```

```python
import jax
import jax.numpy as jnp
from jax import lax
from jax.sharding import Mesh
from jax.sharding import PartitionSpec as P

keep_scale = 10.0 / 9.0
adapter_scale = 0.5

ROW = ("zh", "y")
COL = ("zl", "x", "c")
CHIPS = ("zl", "x")


def dot_f32(left, right):
    return jnp.dot(left, right, preferred_element_type=jnp.float32)


def dot_left_t(left, right):
    return lax.dot_general(
        left, right, (((0,), (0,)), ((), ())), preferred_element_type=jnp.float32
    )


def dot_right_t(left, right):
    return lax.dot_general(
        left, right, (((1,), (1,)), ((), ())), preferred_element_type=jnp.float32
    )


def exchange(blocks, axes):
    return lax.all_to_all(blocks, axes, 0, 0, tiled=True)


def spread(block, axes, count):
    return exchange(jnp.broadcast_to(block[None], (count, *block.shape)), axes)


def sum_blocks(blocks):
    return jnp.sum(blocks.astype(jnp.float32), axis=0)


def trade(value, axis, bit):
    size = lax.axis_size(axis)
    return lax.ppermute(value, axis, [(i, i ^ bit) for i in range(size)])


def shift(value, axis, step):
    size = lax.axis_size(axis)
    return lax.ppermute(value, axis, [(i, (i + step) % size) for i in range(size)])


def sum_pairs(value, steps):
    for axis, bit in steps:
        both = value.astype(jnp.float32) + trade(value, axis, bit).astype(jnp.float32)
        value = both.astype(value.dtype)
    return value


def sum_x(value):
    near, across, far = (shift(value, "x", step).astype(jnp.float32) for step in (-1, 2, 1))
    return ((value.astype(jnp.float32) + across) + (near + far)).astype(value.dtype)


def sum_col(value):
    return sum_pairs(sum_x(sum_pairs(value, (("c", 1),))), (("zl", 1),))


ROW_PAIRS = (("y", 1), ("y", 2), ("zh", 1))
COL_PAIRS = (("c", 1), ("x", 1), ("x", 2), ("zl", 1))


def put(buffer, piece, index, axis, column=0):
    start = [0] * buffer.ndim
    start[axis], start[-1] = index, column
    return lax.dynamic_update_slice(buffer, jnp.expand_dims(piece, axis), start)


def gather_y(piece, axis):
    y, size = lax.axis_index("y"), lax.axis_size("y")
    half = piece.shape[-1] // 2
    behind, ahead = shift(piece, "y", 1), shift(piece, "y", -1)
    return gathered_y(piece, behind, ahead, axis)


def gathered_y(piece, behind, ahead, axis):
    half = piece.shape[-1] // 2
    left = shift(behind[..., :half], "y", 1)
    right = shift(ahead[..., half:], "y", -1)
    return placed_y(piece, behind, ahead, left, right, axis)


def placed_y(piece, behind, ahead, left, right, axis):
    y, size = lax.axis_index("y"), lax.axis_size("y")
    half = piece.shape[-1] // 2
    shape = list(piece.shape)
    shape.insert(axis, size)
    buffer = jnp.zeros(shape, piece.dtype)
    buffer = put(buffer, piece, y, axis)
    buffer = put(buffer, behind, (y + 3) % size, axis)
    buffer = put(buffer, ahead, (y + 1) % size, axis)
    buffer = put(buffer, left, (y + 2) % size, axis)
    return put(buffer, right, (y + 2) % size, axis, half)


def pick_y(array, offset):
    y, size = lax.axis_index("y"), lax.axis_size("y")
    return lax.dynamic_index_in_dim(array, (y + offset) % size, 1, False)


def add(*terms):
    return sum(term.astype(jnp.float32) for term in terms)


def scatter_y_first(first, second):
    return (
        shift(pick_y(first, 2), "y", 1),
        shift(pick_y(second, 2), "y", -1),
        shift(pick_y(first, 3), "y", -1),
        shift(pick_y(second, 1), "y", 1),
    )


def scatter_y_last(first, second, arrived):
    passed_up, passed_down, first_down, second_up = arrived
    first_up = shift(add(pick_y(first, 1), passed_up).astype(first.dtype), "y", 1)
    second_down = shift(add(pick_y(second, 3), passed_down).astype(second.dtype), "y", -1)
    return (
        add(pick_y(first, 0), first_down, first_up),
        add(pick_y(second, 0), second_up, second_down),
    )


def scatter_zh(total):
    zh = lax.axis_index("zh")
    away = lax.dynamic_index_in_dim(total, 1 - zh, 0, False).astype(jnp.bfloat16)
    own = lax.dynamic_index_in_dim(total, zh, 0, False)
    return own + trade(away, "zh", 1).astype(jnp.float32)


def pieces_x(piece):
    return [piece, *[shift(piece, "x", step) for step in (-1, 2, 1)]]


def gather_col(near, far):
    zl, core, x = (lax.axis_index(name) for name in ("zl", "c", "x"))
    size, block = len(near), near[0].shape
    buffer = jnp.zeros((2, size, 2, *block), near[0].dtype)
    for pieces, level in ((near, zl), (far, 1 - zl)):
        rows = jnp.zeros((size, *block), near[0].dtype)
        for offset, piece in enumerate(pieces):
            rows = put(rows, piece, (x + offset) % size, 0)
        for half, side in ((rows, core), (trade(rows, "c", 1), 1 - core)):
            update = half[None, :, None]
            buffer = lax.dynamic_update_slice(buffer, update, (level, 0, side, 0, 0))
    return buffer


def join_zh(piece, axis):
    zh = lax.axis_index("zh")
    shape = list(piece.shape)
    shape.insert(axis, 2)
    other = trade(piece, "zh", 1)
    buffer = put(jnp.zeros(shape, piece.dtype), piece, zh, axis)
    return put(buffer, other, 1 - zh, axis)


def local(tokens, mask, w_gate, w_up, w_down, a_in, a_out, out_grad):
    bf16, f32 = jnp.bfloat16, jnp.float32
    core = lax.axis_index("c")
    row_index = lax.axis_index(ROW)
    chip_index = lax.axis_index(CHIPS)
    col_index = lax.axis_index(COL)
    rank = a_out.shape[1]
    hidden_width = w_gate.shape[1]
    col_tokens, features = tokens.shape
    n_col, n_row = lax.axis_size(COL), lax.axis_size(ROW)
    n_chips = n_col // 2
    all_tokens = col_tokens * n_col
    row_tokens = all_tokens // n_row

    dropped = tokens * mask.astype(bf16)
    low_part = dot_right_t(dropped, a_in) * keep_scale
    low_high = low_part.astype(bf16)
    low_rest = (low_part - low_high.astype(f32)).astype(bf16)
    spare = 128 - 4 * rank
    widened = jnp.concatenate(
        [tokens, low_high, low_rest, jnp.zeros((col_tokens, spare), bf16)], axis=1
    )
    own_side = spread(widened, CHIPS, n_chips)
    other_side = trade(own_side, "c", 1)
    tokens_all = jnp.stack(
        [jnp.where(core == 0, own_side, other_side), jnp.where(core == 0, other_side, own_side)],
        axis=1,
    ).reshape(all_tokens, -1)

    def widen(weight, which):
        maps = jnp.zeros((2 * rank, hidden_width), bf16)
        maps = lax.dynamic_update_slice(maps, a_out[which] * adapter_scale, (which * rank, 0))
        return jnp.concatenate([weight, maps, maps, jnp.zeros((spare, hidden_width), bf16)], axis=0)

    near = pieces_x(out_grad)
    far = pieces_x(trade(out_grad, "zl", 1))
    w_gate_wide, w_up_wide = widen(w_gate, 0), widen(w_up, 1)
    blocks = (2, n_row // 2, row_tokens)
    gate_part = dot_f32(tokens_all, w_gate_wide).astype(bf16).reshape(*blocks, hidden_width)
    gate_part, near, far = lax.optimization_barrier((gate_part, near, far))
    up_part = dot_f32(tokens_all, w_up_wide).astype(bf16).reshape(*blocks, hidden_width)
    low_all = tokens_all[:, features : features + 4 * rank]
    low_all = low_all[:, : 2 * rank].astype(f32) + low_all[:, 2 * rank :].astype(f32)
    low_all = low_all.astype(bf16).reshape(-1, 128)
    gate_up_arrived = scatter_y_first(gate_part, up_part)
    out_grad_all = gather_col(near, far).reshape(all_tokens, features)
    grad_part = dot_right_t(out_grad_all, w_down).astype(bf16).reshape(*blocks, hidden_width)
    gate_up_arrived, grad_part, low_all = lax.optimization_barrier(
        (gate_up_arrived, grad_part, low_all)
    )
    gate_sum, up_sum = scatter_y_last(gate_part, up_part, gate_up_arrived)
    middle = hidden_width // 2
    grad_halves = grad_part[..., :middle], grad_part[..., middle:]
    grad_sums = scatter_y_last(*grad_halves, scatter_y_first(*grad_halves))
    grad_sums = [scatter_zh(total) for total in grad_sums]

    gate, up = scatter_zh(gate_sum), scatter_zh(up_sum)
    sig = jax.nn.sigmoid(gate)
    act = gate * sig
    hidden = (act * up).astype(bf16)

    def by_core(blocks):
        away = lax.dynamic_index_in_dim(blocks, 1 - core, -3, False)
        own = lax.dynamic_index_in_dim(blocks, core, -3, False)
        return jnp.stack([away, own])

    hidden_own = by_core(hidden.reshape(2, col_tokens, -1))
    hidden_behind, hidden_ahead = shift(hidden_own, "y", 1), shift(hidden_own, "y", -1)
    grad_sums, hidden_behind, hidden_ahead = lax.optimization_barrier(
        (grad_sums, hidden_behind, hidden_ahead)
    )
    hidden_grad = jnp.concatenate(grad_sums, axis=1)
    gate_grad = (hidden_grad * up * sig * (1.0 + gate * (1.0 - sig))).astype(bf16)
    up_grad = (hidden_grad * act).astype(bf16)
    joined = jnp.concatenate([gate_grad, up_grad], axis=1)

    low_grad = adapter_scale * jnp.concatenate(
        [dot_right_t(gate_grad, a_out[0]), dot_right_t(up_grad, a_out[1])], axis=1
    )
    low_grad = low_grad.reshape(2, -1, 128)
    zh, y, x = (lax.axis_index(name) for name in ("zh", "y", "x"))
    along_y = jnp.stack([low_grad, *[shift(low_grad, "y", step) for step in (-1, 2, 1)]])
    low_grad = jnp.stack([along_y, trade(along_y, "zh", 1)])
    grads_pair = join_zh(by_core(joined.reshape(2, col_tokens, -1)), 1)
    hidden_y = gathered_y(hidden_own, hidden_behind, hidden_ahead, 1)
    grads_pair, low_grad, hidden_y = lax.optimization_barrier((grads_pair, low_grad, hidden_y))
    grads_behind, grads_ahead = shift(grads_pair, "y", 1), shift(grads_pair, "y", -1)
    def choose(array, index, axis):
        return lax.dynamic_index_in_dim(array, index, axis, False)

    low_grad = choose(low_grad, core, 2) + trade(choose(low_grad, 1 - core, 2), "c", 1)
    low_grad = choose(low_grad, (x - y) % 4, 1) + sum(
        shift(choose(low_grad, (x + step - y) % 4, 1), "x", step) for step in (1, 2, 3)
    )
    apart = lax.axis_index("zl") ^ zh
    low_grad = choose(low_grad, apart, 0) + trade(choose(low_grad, 1 - apart, 0), "zl", 1)
    scaled_own = (low_grad * keep_scale).astype(bf16).reshape(col_tokens, 2 * rank)
    hidden_pieces = join_zh(hidden_y, 1)
    grads_behind, grads_ahead, scaled_own, hidden_pieces = lax.optimization_barrier(
        (grads_behind, grads_ahead, scaled_own, hidden_pieces)
    )
    half_tokens = all_tokens // 2
    hidden_halves = hidden_pieces.reshape(2, half_tokens, hidden_width)

    grads_left = shift(grads_behind[..., :hidden_width], "y", 1)
    grads_right = shift(grads_ahead[..., hidden_width:], "y", -1)
    def own_and_away(halves, product):
        return product(halves[1]).astype(bf16), trade(product(halves[0]).astype(bf16), "c", 1)

    def chip_sum(own, away):
        total = (own.astype(f32) + away.astype(f32)).astype(bf16)
        return total.reshape(n_chips, col_tokens, -1)

    mixed_sum = chip_sum(*own_and_away(hidden_halves, lambda rows: dot_f32(rows, w_down)))
    adapt_part = dot_left_t(scaled_own, dropped).astype(bf16)
    last_blocks = jnp.pad(mixed_sum, ((0, 0), (0, col_tokens), (0, 0)))
    grads_left, grads_right, last_blocks = lax.optimization_barrier(
        (grads_left, grads_right, last_blocks)
    )
    grads_pieces = placed_y(grads_pair, grads_behind, grads_ahead, grads_left, grads_right, 2)
    grads_halves = grads_pieces.reshape(2, half_tokens, 2 * hidden_width)

    def back(half):
        gate_term = dot_right_t(half[:, :hidden_width], w_gate)
        return (gate_term + dot_right_t(half[:, hidden_width:], w_up)).astype(bf16)

    frozen_away = trade(back(grads_halves[0]), "c", 1)
    frozen_own = lax.optimization_barrier(back(grads_halves[1]))
    frozen_sum = chip_sum(frozen_own, frozen_away)
    last_blocks = lax.dynamic_update_slice(last_blocks, frozen_sum, (0, col_tokens, 0))
    adapt_part = sum_col(adapt_part)
    last_blocks, low_all, adapt_part = lax.optimization_barrier((last_blocks, low_all, adapt_part))
    last_sum = sum_blocks(exchange(last_blocks, CHIPS))
    grad_adapt_in = adapt_part.astype(f32)
    adapter_part = mask.astype(f32) * dot_f32(scaled_own, a_in)
    mixed_out = last_sum[:col_tokens].astype(bf16)
    token_input_gradient = (last_sum[col_tokens:] + adapter_part).astype(bf16)

    low_all = sum_pairs(low_all, ROW_PAIRS).reshape(all_tokens, 2 * rank)
    low_halves = by_core(low_all.reshape(n_chips, 2, col_tokens, 2 * rank))
    low_rows = low_halves.reshape(all_tokens, 2 * rank)
    grads_rows = grads_halves.reshape(all_tokens, 2 * hidden_width)
    adapter_output_gradient = adapter_scale * jnp.stack(
        [
            dot_left_t(low_rows[:, :rank], grads_rows[:, :hidden_width]),
            dot_left_t(low_rows[:, rank:], grads_rows[:, hidden_width:]),
        ]
    )
    return mixed_out, token_input_gradient, grad_adapt_in, adapter_output_gradient


def solution(mesh):
    split = Mesh(mesh.devices.reshape(2, 4, 2, 4, 2), (*ROW, *COL))
    both = P(COL, ROW)
    return jax.shard_map(
        local,
        mesh=split,
        in_specs=(
            both,
            both,
            P(ROW, COL),
            P(ROW, COL),
            both,
            P(None, ROW),
            P(None, None, COL),
            both,
        ),
        out_specs=(both, both, P(None, ROW), P(None, None, COL)),
        check_vma=False,
    )
```

```python
import jax
import jax.numpy as jnp
from jax import lax
from jax.sharding import Mesh
from jax.sharding import PartitionSpec as P

keep_scale = 10.0 / 9.0
adapter_scale = 0.5

ROW = ("zh", "y")
COL = ("zl", "x", "c")
CHIPS = ("zl", "x")


def dot_f32(left, right):
    return jnp.dot(left, right, preferred_element_type=jnp.float32)


def dot_left_t(left, right):
    return lax.dot_general(
        left, right, (((0,), (0,)), ((), ())), preferred_element_type=jnp.float32
    )


def dot_right_t(left, right):
    return lax.dot_general(
        left, right, (((1,), (1,)), ((), ())), preferred_element_type=jnp.float32
    )


def exchange(blocks, axes):
    return lax.all_to_all(blocks, axes, 0, 0, tiled=True)


def spread(block, axes, count):
    return exchange(jnp.broadcast_to(block[None], (count, *block.shape)), axes)


def sum_blocks(blocks):
    return jnp.sum(blocks.astype(jnp.float32), axis=0)


def trade(value, axis, bit):
    size = lax.axis_size(axis)
    return lax.ppermute(value, axis, [(i, i ^ bit) for i in range(size)])


def shift(value, axis, step):
    size = lax.axis_size(axis)
    return lax.ppermute(value, axis, [(i, (i + step) % size) for i in range(size)])


def sum_pairs(value, steps):
    for axis, bit in steps:
        both = value.astype(jnp.float32) + trade(value, axis, bit).astype(jnp.float32)
        value = both.astype(value.dtype)
    return value


def sum_x(value):
    near, across, far = (shift(value, "x", step).astype(jnp.float32) for step in (-1, 2, 1))
    return ((value.astype(jnp.float32) + across) + (near + far)).astype(value.dtype)


ROW_PAIRS = (("y", 1), ("y", 2), ("zh", 1))
COL_PAIRS = (("c", 1), ("x", 1), ("x", 2), ("zl", 1))


def put(buffer, piece, index, axis, column=0):
    start = [0] * buffer.ndim
    start[axis], start[-1] = index, column
    return lax.dynamic_update_slice(buffer, jnp.expand_dims(piece, axis), start)


def gather_y(piece, axis):
    y, size = lax.axis_index("y"), lax.axis_size("y")
    half = piece.shape[-1] // 2
    behind, ahead = shift(piece, "y", 1), shift(piece, "y", -1)
    return gathered_y(piece, behind, ahead, axis)


def gathered_y(piece, behind, ahead, axis):
    half = piece.shape[-1] // 2
    left = shift(behind[..., :half], "y", 1)
    right = shift(ahead[..., half:], "y", -1)
    return placed_y(piece, behind, ahead, left, right, axis)


def placed_y(piece, behind, ahead, left, right, axis):
    y, size = lax.axis_index("y"), lax.axis_size("y")
    half = piece.shape[-1] // 2
    shape = list(piece.shape)
    shape.insert(axis, size)
    buffer = jnp.zeros(shape, piece.dtype)
    buffer = put(buffer, piece, y, axis)
    buffer = put(buffer, behind, (y + 3) % size, axis)
    buffer = put(buffer, ahead, (y + 1) % size, axis)
    buffer = put(buffer, left, (y + 2) % size, axis)
    return put(buffer, right, (y + 2) % size, axis, half)


def pick_y(array, offset):
    y, size = lax.axis_index("y"), lax.axis_size("y")
    return lax.dynamic_index_in_dim(array, (y + offset) % size, 1, False)


def add(*terms):
    return sum(term.astype(jnp.float32) for term in terms)


def scatter_y_first(first, second):
    return (
        shift(pick_y(first, 2), "y", 1),
        shift(pick_y(second, 2), "y", -1),
        shift(pick_y(first, 3), "y", -1),
        shift(pick_y(second, 1), "y", 1),
    )


def scatter_y_last(first, second, arrived):
    passed_up, passed_down, first_down, second_up = arrived
    first_up = shift(add(pick_y(first, 1), passed_up).astype(first.dtype), "y", 1)
    second_down = shift(add(pick_y(second, 3), passed_down).astype(second.dtype), "y", -1)
    return (
        add(pick_y(first, 0), first_down, first_up),
        add(pick_y(second, 0), second_up, second_down),
    )


def scatter_zh(total):
    zh = lax.axis_index("zh")
    away = lax.dynamic_index_in_dim(total, 1 - zh, 0, False).astype(jnp.bfloat16)
    own = lax.dynamic_index_in_dim(total, zh, 0, False)
    return own + trade(away, "zh", 1).astype(jnp.float32)


def pieces_x(piece):
    return [piece, *[shift(piece, "x", step) for step in (-1, 2, 1)]]


def gather_col(near, far):
    zl, core, x = (lax.axis_index(name) for name in ("zl", "c", "x"))
    size, block = len(near), near[0].shape
    buffer = jnp.zeros((2, size, 2, *block), near[0].dtype)
    for pieces, level in ((near, zl), (far, 1 - zl)):
        rows = jnp.zeros((size, *block), near[0].dtype)
        for offset, piece in enumerate(pieces):
            rows = put(rows, piece, (x + offset) % size, 0)
        for half, side in ((rows, core), (trade(rows, "c", 1), 1 - core)):
            update = half[None, :, None]
            buffer = lax.dynamic_update_slice(buffer, update, (level, 0, side, 0, 0))
    return buffer


def join_zh(piece, axis):
    zh = lax.axis_index("zh")
    shape = list(piece.shape)
    shape.insert(axis, 2)
    other = trade(piece, "zh", 1)
    buffer = put(jnp.zeros(shape, piece.dtype), piece, zh, axis)
    return put(buffer, other, 1 - zh, axis)


def local(tokens, mask, w_gate, w_up, w_down, a_in, a_out, out_grad):
    bf16, f32 = jnp.bfloat16, jnp.float32
    core = lax.axis_index("c")
    row_index = lax.axis_index(ROW)
    chip_index = lax.axis_index(CHIPS)
    col_index = lax.axis_index(COL)
    rank = a_out.shape[1]
    hidden_width = w_gate.shape[1]
    col_tokens, features = tokens.shape
    n_col, n_row = lax.axis_size(COL), lax.axis_size(ROW)
    n_chips = n_col // 2
    all_tokens = col_tokens * n_col
    row_tokens = all_tokens // n_row

    dropped = tokens * mask.astype(bf16)
    low_part = dot_right_t(dropped, a_in) * keep_scale
    low_high = low_part.astype(bf16)
    low_rest = (low_part - low_high.astype(f32)).astype(bf16)
    spare = 128 - 4 * rank
    widened = jnp.concatenate(
        [tokens, low_high, low_rest, jnp.zeros((col_tokens, spare), bf16)], axis=1
    )
    own_side = spread(widened, CHIPS, n_chips)
    other_side = trade(own_side, "c", 1)
    tokens_all = jnp.stack(
        [jnp.where(core == 0, own_side, other_side), jnp.where(core == 0, other_side, own_side)],
        axis=1,
    ).reshape(all_tokens, -1)

    def widen(weight, which):
        maps = jnp.zeros((2 * rank, hidden_width), bf16)
        maps = lax.dynamic_update_slice(maps, a_out[which] * adapter_scale, (which * rank, 0))
        return jnp.concatenate([weight, maps, maps, jnp.zeros((spare, hidden_width), bf16)], axis=0)

    near = pieces_x(out_grad)
    far = pieces_x(trade(out_grad, "zl", 1))
    w_gate_wide, w_up_wide = widen(w_gate, 0), widen(w_up, 1)
    blocks = (2, n_row // 2, row_tokens)
    gate_part = dot_f32(tokens_all, w_gate_wide).astype(bf16).reshape(*blocks, hidden_width)
    up_part = dot_f32(tokens_all, w_up_wide).astype(bf16).reshape(*blocks, hidden_width)
    up_part, near, far = lax.optimization_barrier((up_part, near, far))
    low_all = tokens_all[:, features : features + 4 * rank]
    low_all = low_all[:, : 2 * rank].astype(f32) + low_all[:, 2 * rank :].astype(f32)
    low_all = low_all.astype(bf16).reshape(-1, 128)
    gate_up_arrived = scatter_y_first(gate_part, up_part)
    out_grad_all = gather_col(near, far).reshape(all_tokens, features)
    grad_part = dot_right_t(out_grad_all, w_down).astype(bf16).reshape(*blocks, hidden_width)
    gate_up_arrived, grad_part, low_all = lax.optimization_barrier(
        (gate_up_arrived, grad_part, low_all)
    )
    gate_sum, up_sum = scatter_y_last(gate_part, up_part, gate_up_arrived)
    middle = hidden_width // 2
    grad_halves = grad_part[..., :middle], grad_part[..., middle:]
    grad_sums = scatter_y_last(*grad_halves, scatter_y_first(*grad_halves))
    grad_sums = [scatter_zh(total) for total in grad_sums]

    gate, up = scatter_zh(gate_sum), scatter_zh(up_sum)
    sig = jax.nn.sigmoid(gate)
    act = gate * sig
    hidden = (act * up).astype(bf16)

    def by_core(blocks):
        away = lax.dynamic_index_in_dim(blocks, 1 - core, -3, False)
        own = lax.dynamic_index_in_dim(blocks, core, -3, False)
        return jnp.stack([away, own])

    hidden_own = by_core(hidden.reshape(2, col_tokens, -1))
    hidden_behind, hidden_ahead = shift(hidden_own, "y", 1), shift(hidden_own, "y", -1)
    grad_sums, hidden_behind, hidden_ahead = lax.optimization_barrier(
        (grad_sums, hidden_behind, hidden_ahead)
    )
    hidden_grad = jnp.concatenate(grad_sums, axis=1)
    gate_grad = (hidden_grad * up * sig * (1.0 + gate * (1.0 - sig))).astype(bf16)
    up_grad = (hidden_grad * act).astype(bf16)
    joined = jnp.concatenate([gate_grad, up_grad], axis=1)

    low_grad = adapter_scale * jnp.concatenate(
        [dot_right_t(gate_grad, a_out[0]), dot_right_t(up_grad, a_out[1])], axis=1
    )
    low_grad = low_grad.reshape(2, -1, 128)
    zh, y, x = (lax.axis_index(name) for name in ("zh", "y", "x"))
    along_y = jnp.stack([low_grad, *[shift(low_grad, "y", step) for step in (-1, 2, 1)]])
    low_grad = jnp.stack([along_y, trade(along_y, "zh", 1)])
    grads_pair = join_zh(by_core(joined.reshape(2, col_tokens, -1)), 1)
    hidden_y = gathered_y(hidden_own, hidden_behind, hidden_ahead, 1)
    grads_pair, low_grad, hidden_y = lax.optimization_barrier((grads_pair, low_grad, hidden_y))
    grads_behind, grads_ahead = shift(grads_pair, "y", 1), shift(grads_pair, "y", -1)
    def choose(array, index, axis):
        return lax.dynamic_index_in_dim(array, index, axis, False)

    low_grad = choose(low_grad, core, 2) + trade(choose(low_grad, 1 - core, 2), "c", 1)
    low_grad = choose(low_grad, (x - y) % 4, 1) + sum(
        shift(choose(low_grad, (x + step - y) % 4, 1), "x", step) for step in (1, 2, 3)
    )
    apart = lax.axis_index("zl") ^ zh
    low_grad = choose(low_grad, apart, 0) + trade(choose(low_grad, 1 - apart, 0), "zl", 1)
    scaled_own = (low_grad * keep_scale).astype(bf16).reshape(col_tokens, 2 * rank)
    hidden_pieces = join_zh(hidden_y, 1)
    grads_behind, grads_ahead, scaled_own, hidden_pieces = lax.optimization_barrier(
        (grads_behind, grads_ahead, scaled_own, hidden_pieces)
    )
    half_tokens = all_tokens // 2
    hidden_halves = hidden_pieces.reshape(2, half_tokens, hidden_width)

    grads_left = shift(grads_behind[..., :hidden_width], "y", 1)
    grads_right = shift(grads_ahead[..., hidden_width:], "y", -1)
    def own_and_away(halves, product):
        return product(halves[1]).astype(bf16), trade(product(halves[0]).astype(bf16), "c", 1)

    def chip_sum(own, away):
        total = (own.astype(f32) + away.astype(f32)).astype(bf16)
        return total.reshape(n_chips, col_tokens, -1)

    mixed_sum = chip_sum(*own_and_away(hidden_halves, lambda rows: dot_f32(rows, w_down)))
    adapt_part = dot_left_t(scaled_own, dropped).astype(bf16)
    last_blocks = jnp.pad(mixed_sum, ((0, 0), (0, col_tokens), (0, 0)))
    grads_left, grads_right, last_blocks = lax.optimization_barrier(
        (grads_left, grads_right, last_blocks)
    )
    grads_pieces = placed_y(grads_pair, grads_behind, grads_ahead, grads_left, grads_right, 2)
    grads_halves = grads_pieces.reshape(2, half_tokens, 2 * hidden_width)

    def back(half):
        gate_term = dot_right_t(half[:, :hidden_width], w_gate)
        return (gate_term + dot_right_t(half[:, hidden_width:], w_up)).astype(bf16)

    frozen_away = trade(back(grads_halves[0]), "c", 1)
    adapt_part = sum_x(sum_pairs(adapt_part, (("c", 1),)))
    frozen_own, adapt_part = lax.optimization_barrier((back(grads_halves[1]), adapt_part))
    frozen_sum = chip_sum(frozen_own, frozen_away)
    last_blocks = lax.dynamic_update_slice(last_blocks, frozen_sum, (0, col_tokens, 0))
    adapt_part = sum_pairs(adapt_part, (("zl", 1),))
    last_blocks, low_all, adapt_part = lax.optimization_barrier((last_blocks, low_all, adapt_part))
    last_sum = sum_blocks(exchange(last_blocks, CHIPS))
    grad_adapt_in = adapt_part.astype(f32)
    adapter_part = mask.astype(f32) * dot_f32(scaled_own, a_in)
    mixed_out = last_sum[:col_tokens].astype(bf16)
    token_input_gradient = (last_sum[col_tokens:] + adapter_part).astype(bf16)

    low_all = sum_pairs(low_all, ROW_PAIRS).reshape(all_tokens, 2 * rank)
    low_halves = by_core(low_all.reshape(n_chips, 2, col_tokens, 2 * rank))
    low_rows = low_halves.reshape(all_tokens, 2 * rank)
    grads_rows = grads_halves.reshape(all_tokens, 2 * hidden_width)
    adapter_output_gradient = adapter_scale * jnp.stack(
        [
            dot_left_t(low_rows[:, :rank], grads_rows[:, :hidden_width]),
            dot_left_t(low_rows[:, rank:], grads_rows[:, hidden_width:]),
        ]
    )
    return mixed_out, token_input_gradient, grad_adapt_in, adapter_output_gradient


def solution(mesh):
    split = Mesh(mesh.devices.reshape(2, 4, 2, 4, 2), (*ROW, *COL))
    both = P(COL, ROW)
    return jax.shard_map(
        local,
        mesh=split,
        in_specs=(
            both,
            both,
            P(ROW, COL),
            P(ROW, COL),
            both,
            P(None, ROW),
            P(None, None, COL),
            both,
        ),
        out_specs=(both, both, P(None, ROW), P(None, None, COL)),
        check_vma=False,
    )
```
